32 devices in a mesh: ctx: 8 (over z, core), head: 4 (over y, x).
Axes of the slice: x: 2, y: 2, z: 4, core: 2. Of those that a mesh axis runs over, the one named last changes fastest.
Arguments:
- queries: bfloat16 [4096, 8192], P('ctx', 'head'), may hold values from -136 to 136
- keys: bfloat16 [4096, 8192], P('ctx', 'head'), may hold values from -6 to 6
- values: bfloat16 [4096, 8192], P('ctx', 'head'), may hold values from -6 to 6
- segment_ids: int32 [4096], P('ctx'), may hold values from 0 to 3, never falling along the last dimension, each value on 1 to 2048 neighbouring positions
Outputs:
- attended: bfloat16 [4096, 8192], P('ctx', 'head')
The draws below stay inside these ranges and needn't reach their ends.
Inputs may be any that keep to these rules, and one draw needn't show every extreme that they name: `segment_ids`: document numbers never fall along the tokens; every document of 0 to 3 appears, with 1 to 2048 tokens, one with exactly 2048.
All inputs are finite; a program needn't handle non-finite values.
Results may differ from the reference program's by a relative error of at most 0.0049.
Values may be sent and summed in bfloat16 or wider, within the bound.
A program may use at most 64 MiB of HBM per device.

```python
import math
import jax
import jax.numpy as jnp
import numpy as np
from jax import lax

HEADS = 64
DH = 128
BLK = 512
DOCS = 4
TOKENS = 4096
SEG_MOST = 2048


def draw_queries(key, part):
    key_base = jax.random.fold_in(key, 11)
    key_head = jax.random.fold_in(key, 12)
    head_scale = jnp.exp(jax.random.uniform(key_head, (HEADS,), jnp.float32) * math.log(10.0))
    base = jnp.clip(jax.random.normal(key_base, (TOKENS, HEADS, DH), jnp.float32), -6.0, 6.0)
    full = base * head_scale[None, :, None]
    return full.reshape(TOKENS, HEADS * DH).astype(jnp.bfloat16)


def block_levels(key, dims, cuts, smallest, largest):
    gain, own = 1.0, jax.random.fold_in(key, 6)
    for dim, shards_of in cuts:
        steps = jnp.exp(jax.random.uniform(jax.random.fold_in(own, dim), (shards_of,), jnp.float32, smallest / len(cuts), largest / len(cuts)))
        gain = gain * jnp.repeat(steps, dims[dim] // shards_of).reshape([-1 if axis == dim else 1 for axis in range(len(dims))])
    return gain


def profile(number_of, total, reach, skew):
    portions = [(1 << 20) // math.isqrt(standing ** skew) + 1 for standing in range(2, number_of + 1)]
    rest, holding = total - reach - (number_of - 1), [1] * (number_of - 1)
    while rest > 0:
        free = [i for i in range(number_of - 1) if holding[i] < reach]
        pool, budget = sum([portions[i] for i in free]), rest
        for i in free:
            addition = min(reach - holding[i], max(1, budget * portions[i] // pool), rest)
            holding[i] = holding[i] + addition
            rest = rest - addition
    return np.array([reach] + holding)


def ragged(stream_key, amount, total, reach, slope):
    if amount == 2:
        one = jax.random.randint(stream_key, (), max(1, total - reach), min(reach, total - 1) + 1)
        return jnp.stack([one, total - one])
    lengths = jnp.asarray(profile(amount, total, reach, slope), jnp.int32)
    couples = (amount - 1) // 2
    donor, sink = lengths[1:1 + 2 * couples:2], lengths[2:2 + 2 * couples:2]
    slack = jnp.minimum(donor - 1, reach - sink)
    moved = jax.random.randint(jax.random.fold_in(stream_key, 1), (couples,), 0, 1 << 20) % (slack + 1)
    lengths = lengths.at[1:1 + 2 * couples:2].set(donor - moved).at[2:2 + 2 * couples:2].set(sink + moved)
    return lengths[jax.random.permutation(jax.random.fold_in(stream_key, 2), amount)]


def normal_values(rng, extent, width, limit, shards=(), held_as=jnp.bfloat16):
    result = jax.random.normal(rng, extent, jnp.float32) * width
    if len(shards) > 0:
        result = block_levels(rng, extent, shards, -0.22, 0.18) * result
    return jnp.clip(result, min=-limit, max=limit).astype(held_as)


def setup_inputs(seed: int = 0) -> dict:
    key_of = jax.random.split(jax.random.key(seed), 5)
    return {
        "queries": draw_queries(jax.random.fold_in(key_of[4], 71), 0),
        "keys": normal_values(key_of[1], (TOKENS, HEADS * DH), 1.0, 6.0, ((0, 8), (1, 4))),
        "values": normal_values(key_of[2], (TOKENS, HEADS * DH), 1.0, 6.0, ((0, 8), (1, 4))),
        "segment_ids": jnp.searchsorted(jnp.cumsum(ragged(key_of[3], DOCS, TOKENS, SEG_MOST, 0)), jnp.arange(TOKENS), side="right").astype(jnp.int32),
    }


def reference(queries, keys, values, segment_ids):
    blocks = TOKENS // BLK
    q_all = queries.reshape(blocks, BLK, HEADS, DH)
    k_all = keys.reshape(blocks, BLK, HEADS, DH)
    v_all = values.reshape(blocks, BLK, HEADS, DH)
    s_all = segment_ids.reshape(blocks, BLK)
    rows = jnp.arange(BLK)
    causal = rows[:, None] >= rows[None, :]

    def step(carry, item):
        state, last = carry
        qb, kb, vb, sb = item
        scores = jnp.einsum('thd,shd->hts', qb.astype(jnp.float32), kb.astype(jnp.float32))
        mask = causal & (sb[:, None] == sb[None, :])
        probs = jnp.where(mask[None], scores, 0.0).astype(jnp.bfloat16)
        intra = jnp.einsum('hts,shd->thd', probs.astype(jnp.float32), vb.astype(jnp.float32))
        state_b = state.astype(jnp.bfloat16).astype(jnp.float32)
        inter = jnp.einsum('thd,hde->the', qb.astype(jnp.float32), state_b)
        inter = jnp.where((sb == last)[:, None, None], inter, 0.0)
        block_last = sb[-1]
        keep = (sb == block_last)[:, None, None]
        kv = jnp.einsum('thd,the->hde', jnp.where(keep, kb, jnp.zeros_like(kb)).astype(jnp.float32), vb.astype(jnp.float32))
        new_state = jnp.where(last == block_last, state, jnp.zeros_like(state)) + kv
        return ((new_state, block_last), intra + inter)
    init = (jnp.zeros((HEADS, DH, DH), jnp.float32), jnp.int32(-1))
    _, outs = lax.scan(step, init, (q_all, k_all, v_all, s_all))
    outs = outs.reshape(TOKENS, HEADS * DH)
    mean_sq = lax.optimization_barrier(jnp.sum(outs * outs, axis=1)) / (HEADS * DH)
    return (outs * lax.rsqrt(mean_sq + 1e-05)[:, None]).astype(jnp.bfloat16)
```

```python
import functools

import jax
import jax.numpy as jnp
from jax import lax
from jax.experimental import pallas as pl
from jax.experimental.pallas import tpu as pltpu
from jax.sharding import PartitionSpec as P

DH = 128
EPS = 1e-05
F32 = jnp.float32
BF16 = jnp.bfloat16
MESH = pl.DeviceIdType.MESH


def dot(a, b, dims):
    return lax.dot_general(a, b, (dims, ((), ())), preferred_element_type=F32)


def kernel(
    n_ctx, n_head,
    q_hbm, k_hbm, v_hbm, seg_ref, out_ref,
    q, k, v, o, mask, keep, seg_col, sq,
    kv_own, kv_send, kv_rcv, p_rcv, p_send, sb_own, sb_send, sb_rcv,
    tag_own, tag_partner, tag_odd, tag_prev, ss,
    in_sem, kv_ssem, kv_rsem, p_ssem, p_rsem, sb_ssem, sb_rsem, tag_ssem, tag_rsem, ss_ssem, ss_rsem,
):
    heads, rows, _ = q.shape
    hc = heads // 2
    half = rows // 2
    chips = n_ctx // 2
    ctx = lax.axis_index("ctx")
    me = lax.axis_index("head")
    core = ctx % 2
    chip = ctx // 2
    even = core == 0
    partner = ctx + 1 - 2 * core
    first, last = chip == 0, chip == chips - 1
    mine, other = core * hc, (1 - core) * hc

    def load(which, h):
        src, dst = ((k_hbm, k), (v_hbm, v), (q_hbm, q))[which]
        cols = pl.ds(pl.multiple_of(h * DH, DH), DH)
        return pltpu.make_async_copy(src.at[:, cols], dst.at[h], in_sem.at[which, h])

    def remote(src, dst, ssem, rsem, where):
        return pltpu.make_async_remote_copy(
            src_ref=src, dst_ref=dst, send_sem=ssem, recv_sem=rsem, device_id=where, device_id_type=MESH
        )

    def kv_copy(j):
        return remote(kv_send.at[j], kv_rcv.at[j], kv_ssem.at[j], kv_rsem.at[j], {"ctx": partner})

    def p_copy(j):
        return remote(p_send.at[j], p_rcv.at[j], p_ssem.at[j], p_rsem.at[j], {"ctx": ctx + 2})

    def sb_copy(j):
        return remote(sb_send.at[j], sb_rcv.at[j], sb_ssem.at[j], sb_rsem.at[j], {"ctx": partner})

    tag_pair = remote(tag_own, tag_partner, tag_ssem.at[0], tag_rsem.at[0], {"ctx": partner})
    tag_next = remote(tag_odd, tag_prev, tag_ssem.at[1], tag_rsem.at[1], {"ctx": ctx + 2})

    def ss_copy(d):
        return remote(ss.at[0], ss.at[d], ss_ssem.at[d], ss_rsem.at[d], {"head": lax.rem(me + d, n_head)})

    @pl.loop(0, hc)
    def _(j):
        for base in (other, mine):
            load(0, base + j).start()
            load(1, base + j).start()

    @pl.loop(0, heads)
    def _(h):
        load(2, h).start()

    barrier = pltpu.get_barrier_semaphore()
    pl.semaphore_signal(barrier, inc=1, device_id={"ctx": partner}, device_id_type=MESH)
    for d in range(1, n_head):
        pl.semaphore_signal(
            barrier, inc=1, device_id={"head": lax.rem(me + d, n_head)}, device_id_type=MESH
        )

    @pl.when(jnp.logical_not(first))
    def _():
        pl.semaphore_signal(barrier, inc=1, device_id={"ctx": ctx - 2}, device_id_type=MESH)

    @pl.when(jnp.logical_not(last))
    def _():
        pl.semaphore_signal(barrier, inc=1, device_id={"ctx": ctx + 2}, device_id_type=MESH)

    seg_row = seg_ref[...].astype(F32)
    seg_col[...] = jnp.broadcast_to(seg_row, (DH, rows)).T
    col = seg_col[...]
    tail = col[rows - 1:rows, :]
    tag_own[...] = jnp.broadcast_to(tail, tag_own.shape)
    keep[...] = jnp.where(col == tail, 1.0, 0.0).astype(BF16)
    t_at = lax.broadcasted_iota(jnp.int32, (rows, DH), 0)
    s_at = lax.broadcasted_iota(jnp.int32, (rows, DH), 1)
    for c in range(rows // DH):
        cut = slice(c * DH, (c + 1) * DH)
        seen = (col == seg_row[:, cut]) & (t_at >= s_at + c * DH)
        mask[:, cut] = jnp.where(seen, 1.0, 0.0).astype(BF16)
    sq[...] = jnp.zeros_like(sq)

    @pl.when(first)
    def _():
        p_rcv[...] = jnp.zeros_like(p_rcv)
        tag_prev[...] = jnp.full_like(tag_prev, -1.0)

    greeted = n_head + 2 - first.astype(jnp.int32) - last.astype(jnp.int32)
    pl.semaphore_wait(barrier, greeted)
    tag_pair.start()

    def state_of(h):
        load(0, h).wait()
        load(1, h).wait()
        return dot(k[h] * keep[...], v[h], ((0,), (0,)))

    def tag_even_row():
        return jnp.where(even, tag_own[0:1, :], tag_partner[0:1, :])

    def service(j):
        kv_copy(j).wait_recv()

        @pl.when(jnp.logical_not(first))
        def _():
            p_copy(j).wait_recv()

        own, got = kv_own[j], kv_rcv[j]
        kv_even = jnp.where(even, own, got)
        kv_odd = jnp.where(even, got, own)
        t_even = tag_even_row()
        stay_even = jnp.where(tag_prev[0:1, :] == t_even, 1.0, 0.0)
        stay_odd = jnp.where(t_even == tag_odd[0:1, :], 1.0, 0.0)
        before = p_rcv[j].astype(F32)
        middle = before * stay_even + kv_even

        @pl.when(jnp.logical_not(last))
        def _():
            p_send[j] = (middle * stay_odd + kv_odd).astype(p_send.dtype)
            p_copy(j).start()

        sb_own[j] = jnp.where(even, before, middle).astype(BF16)
        sb_send[j] = jnp.where(even, middle, before).astype(BF16)
        sb_copy(j).start()

    def kv_step(j):
        kv_send[j] = state_of(other + j)
        kv_copy(j).start()
        kv_own[j] = state_of(mine + j)

    kv_step(0)
    tag_pair.wait_recv()
    tag_odd[...] = jnp.where(even, tag_partner[...], tag_own[...])

    @pl.when(jnp.logical_not(last))
    def _():
        tag_next.start()

    @pl.loop(1, hc)
    def _(j):
        kv_step(j)

        @pl.when(first)
        def _():
            service(j - 1)

    @pl.when(first)
    def _():
        service(hc - 1)

    @pl.when(jnp.logical_not(first))
    def _():
        tag_next.wait_recv()

    lag = heads // 4

    @pl.loop(0, heads)
    def _(h):
        load(2, h).wait()
        low = dot(q[h, :half, :], k[h, :half, :], ((1,), (1,))).astype(BF16) * mask[:half, :half]
        high = dot(q[h, half:, :], k[h], ((1,), (1,))).astype(BF16) * mask[half:, :]
        o[h, :half, :] = dot(low, v[h, :half, :], ((1,), (0,)))
        o[h, half:, :] = dot(high, v[h], ((1,), (0,)))
        turn = h - lag * chip

        @pl.when(jnp.logical_not(first) & jnp.logical_not(last) & (turn >= 0) & (turn < hc))
        def _():
            service(turn)

    t_last = jnp.where(even, tag_prev[0:1, :], tag_even_row())
    keep[...] = jnp.where(seg_col[...] == t_last, 1.0, 0.0).astype(BF16)

    def add_inter(h, state):
        total = o[h] + dot(q[h] * keep[...], state, ((1,), (0,)))
        o[h] = total
        sq[...] += total * total

    def finish_other(j):
        sb_copy(j).wait_recv()
        add_inter(other + j, sb_rcv[j])

    @pl.loop(0, hc)
    def _(j):
        @pl.when(jnp.logical_not(first) & (last | (lag * chip + j >= heads)))
        def _():
            service(j)

        @pl.when(j > 0)
        def _():
            finish_other(j - 1)

        add_inter(mine + j, sb_own[j])

    finish_other(hc - 1)

    spread = sq[...].T
    ss[0] = jnp.sum(spread.reshape(DH // 8, 8, rows), axis=0)
    for d in range(1, n_head):
        ss_copy(d).start()
    total = ss[0]
    for d in range(1, n_head):
        ss_copy(d).wait_recv()
        total = total + ss[d]
    mean = jnp.sum(total, axis=0, keepdims=True) / (heads * n_head * DH)
    sq[...] = jnp.broadcast_to(lax.rsqrt(mean + EPS), (DH, rows)).T

    for h in range(heads):
        out_ref[:, h * DH:(h + 1) * DH] = (o[h] * sq[...]).astype(BF16)

    tag_pair.wait_send()
    for d in range(1, n_head):
        ss_copy(d).wait_send()

    @pl.when(jnp.logical_not(last))
    def _():
        tag_next.wait_send()

    @pl.loop(0, hc)
    def _(j):
        kv_copy(j).wait_send()
        sb_copy(j).wait_send()

        @pl.when(jnp.logical_not(last))
        def _():
            p_copy(j).wait_send()


def on_device(n_ctx, n_head, queries, keys, values, segment_ids):
    rows, cols = queries.shape
    heads = cols // DH
    hc = heads // 2
    wire = BF16 if n_ctx <= 16 else F32
    vmem, dma = pltpu.VMEM, pltpu.SemaphoreType.DMA
    big = vmem((heads, rows, DH), BF16)
    state = vmem((hc, DH, DH), F32)
    state_p = vmem((hc, DH, DH), wire)
    state_b = vmem((hc, DH, DH), BF16)
    tag = vmem((8, DH), F32)
    anywhere = pl.BlockSpec(memory_space=pl.ANY)
    inside = pl.BlockSpec(memory_space=pltpu.VMEM)
    return pl.pallas_call(
        functools.partial(kernel, n_ctx, n_head),
        out_shape=jax.ShapeDtypeStruct((rows, cols), BF16),
        in_specs=[anywhere, anywhere, anywhere, inside],
        out_specs=inside,
        scratch_shapes=[
            big, big, big,
            vmem((heads, rows, DH), F32),
            vmem((rows, rows), BF16),
            vmem((rows, DH), BF16),
            vmem((rows, DH), F32),
            vmem((rows, DH), F32),
            state, state, state, state_p, state_p, state_b, state_b, state_b,
            tag, tag, tag, tag,
            vmem((n_head, 8, rows), F32),
            dma((3, heads)),
            dma((hc,)), dma((hc,)), dma((hc,)), dma((hc,)), dma((hc,)), dma((hc,)),
            dma((2,)), dma((2,)), dma((n_head,)), dma((n_head,)),
        ],
        compiler_params=pltpu.CompilerParams(
            collective_id=0, has_side_effects=True, vmem_limit_bytes=48 * 2**20
        ),
        cost_estimate=pl.CostEstimate(
            flops=2 * heads * rows * DH * (2 * rows + 2 * DH), bytes_accessed=8 * rows * cols, transcendentals=rows
        ),
    )(queries, keys, values, segment_ids.reshape(1, rows))


def solution(mesh):
    n_ctx, n_head = mesh.shape["ctx"], mesh.shape["head"]
    in_specs = (P("ctx", "head"), P("ctx", "head"), P("ctx", "head"), P("ctx"))
    return jax.shard_map(
        functools.partial(on_device, n_ctx, n_head),
        mesh=mesh, in_specs=in_specs, out_specs=P("ctx", "head"), check_vma=False,
    )
```

```python
import functools

import jax
import jax.numpy as jnp
from jax import lax
from jax.experimental import pallas as pl
from jax.experimental.pallas import tpu as pltpu
from jax.sharding import PartitionSpec as P

DH = 128
EPS = 1e-05
F32 = jnp.float32
BF16 = jnp.bfloat16
MESH = pl.DeviceIdType.MESH


def dot(a, b, dims):
    return lax.dot_general(a, b, (dims, ((), ())), preferred_element_type=F32)


def kernel(
    n_ctx, n_head,
    q_hbm, k_hbm, v_hbm, seg_hbm, out_ref,
    q, k, v, seg, o, mask, keep, seg_col, sq,
    kv_own, kv_send, kv_rcv, p_rcv, p_send, sb_own, sb_send, sb_rcv,
    tag_own, tag_partner, tag_odd, tag_prev, ss,
    in_sem, seg_sem, kv_ssem, kv_rsem, p_ssem, p_rsem, sb_ssem, sb_rsem, tag_ssem, tag_rsem, ss_ssem, ss_rsem,
):
    heads, rows, _ = q.shape
    hc = heads // 2
    half = rows // 2
    chips = n_ctx // 2
    ctx = lax.axis_index("ctx")
    me = lax.axis_index("head")
    core = ctx % 2
    chip = ctx // 2
    even = core == 0
    partner = ctx + 1 - 2 * core
    first, last = chip == 0, chip == chips - 1
    mine, other = core * hc, (1 - core) * hc

    def load(which, h):
        src, dst = ((k_hbm, k), (v_hbm, v), (q_hbm, q))[which]
        cols = pl.ds(pl.multiple_of(h * DH, DH), DH)
        return pltpu.make_async_copy(src.at[:, cols], dst.at[h], in_sem.at[which, h])

    def remote(src, dst, ssem, rsem, where):
        return pltpu.make_async_remote_copy(
            src_ref=src, dst_ref=dst, send_sem=ssem, recv_sem=rsem, device_id=where, device_id_type=MESH
        )

    def kv_copy(j):
        return remote(kv_send.at[j], kv_rcv.at[j], kv_ssem.at[j], kv_rsem.at[j], {"ctx": partner})

    def p_copy(j):
        return remote(p_send.at[j], p_rcv.at[j], p_ssem.at[j], p_rsem.at[j], {"ctx": ctx + 2})

    def sb_copy(j):
        return remote(sb_send.at[j], sb_rcv.at[j], sb_ssem.at[j], sb_rsem.at[j], {"ctx": partner})

    tag_pair = remote(tag_own, tag_partner, tag_ssem.at[0], tag_rsem.at[0], {"ctx": partner})
    tag_next = remote(tag_odd, tag_prev, tag_ssem.at[1], tag_rsem.at[1], {"ctx": ctx + 2})

    def ss_copy(d):
        return remote(ss.at[0], ss.at[d], ss_ssem.at[d], ss_rsem.at[d], {"head": lax.rem(me + d, n_head)})

    seg_load = pltpu.make_async_copy(seg_hbm, seg, seg_sem)
    seg_load.start()

    @pl.loop(0, hc)
    def _(j):
        for base in (other, mine):
            load(0, base + j).start()
            load(1, base + j).start()

    @pl.loop(0, heads)
    def _(h):
        load(2, h).start()

    barrier = pltpu.get_barrier_semaphore()
    pl.semaphore_signal(barrier, inc=1, device_id={"ctx": partner}, device_id_type=MESH)
    for d in range(1, n_head):
        pl.semaphore_signal(
            barrier, inc=1, device_id={"head": lax.rem(me + d, n_head)}, device_id_type=MESH
        )

    @pl.when(jnp.logical_not(first))
    def _():
        pl.semaphore_signal(barrier, inc=1, device_id={"ctx": ctx - 2}, device_id_type=MESH)

    @pl.when(jnp.logical_not(last))
    def _():
        pl.semaphore_signal(barrier, inc=1, device_id={"ctx": ctx + 2}, device_id_type=MESH)

    seg_load.wait()
    seg_row = seg[...].astype(F32)
    seg_col[...] = jnp.broadcast_to(seg_row, (DH, rows)).T
    col = seg_col[...]
    tail = col[rows - 1:rows, :]
    tag_own[...] = jnp.broadcast_to(tail, tag_own.shape)
    keep[...] = jnp.where(col == tail, 1.0, 0.0).astype(BF16)
    t_at = lax.broadcasted_iota(jnp.int32, (rows, DH), 0)
    s_at = lax.broadcasted_iota(jnp.int32, (rows, DH), 1)
    for c in range(rows // DH):
        cut = slice(c * DH, (c + 1) * DH)
        seen = (col == seg_row[:, cut]) & (t_at >= s_at + c * DH)
        mask[:, cut] = jnp.where(seen, 1.0, 0.0).astype(BF16)
    sq[...] = jnp.zeros_like(sq)

    @pl.when(first)
    def _():
        p_rcv[...] = jnp.zeros_like(p_rcv)
        tag_prev[...] = jnp.full_like(tag_prev, -1.0)

    greeted = n_head + 2 - first.astype(jnp.int32) - last.astype(jnp.int32)
    pl.semaphore_wait(barrier, greeted)
    tag_pair.start()

    def tag_even_row():
        return jnp.where(even, tag_own[0:1, :], tag_partner[0:1, :])

    def service(j):
        kv_copy(j).wait_recv()

        @pl.when(jnp.logical_not(first))
        def _():
            p_copy(j).wait_recv()

        own, got = kv_own[j], kv_rcv[j]
        kv_even = jnp.where(even, own, got)
        kv_odd = jnp.where(even, got, own)
        t_even = tag_even_row()
        stay_even = jnp.where(tag_prev[0:1, :] == t_even, 1.0, 0.0)
        stay_odd = jnp.where(t_even == tag_odd[0:1, :], 1.0, 0.0)
        before = p_rcv[j].astype(F32)
        middle = before * stay_even + kv_even

        @pl.when(jnp.logical_not(last))
        def _():
            p_send[j] = (middle * stay_odd + kv_odd).astype(p_send.dtype)
            p_copy(j).start()

        sb_own[j] = jnp.where(even, before, middle).astype(BF16)
        sb_send[j] = jnp.where(even, middle, before).astype(BF16)
        sb_copy(j).start()

    def kv_step(j):
        ahead = [(base + j + i) for i in range(2) for base in (other, mine)]
        for h in ahead:
            load(0, h).wait()
            load(1, h).wait()
        stay = keep[...]
        sums = [dot(k[h] * stay, v[h], ((0,), (0,))) for h in ahead]
        for i in range(2):
            kv_send[j + i] = sums[2 * i]
            kv_own[j + i] = sums[2 * i + 1]
        for i in range(2):
            kv_copy(j + i).start()

    kv_step(0)
    tag_pair.wait_recv()
    tag_odd[...] = jnp.where(even, tag_partner[...], tag_own[...])

    @pl.when(jnp.logical_not(last))
    def _():
        tag_next.start()

    @pl.loop(2, hc, step=2)
    def _(j):
        kv_step(j)

        @pl.when(first)
        def _():
            service(j - 2)
            service(j - 1)

    @pl.when(first)
    def _():
        service(hc - 2)
        service(hc - 1)

    @pl.when(jnp.logical_not(first))
    def _():
        tag_next.wait_recv()

    lag = max(2, heads // 4 // 2 * 2)

    @pl.loop(0, heads, step=2)
    def _(h):
        for i in range(2):
            load(2, h + i).wait()
        tops = [dot(q[h + i, :half, :], k[h + i, :half, :], ((1,), (1,))) for i in range(2)]
        ends = [dot(q[h + i, half:, :], k[h + i], ((1,), (1,))) for i in range(2)]
        tops = [part.astype(BF16) * mask[:half, :half] for part in tops]
        ends = [part.astype(BF16) * mask[half:, :] for part in ends]
        for i in range(2):
            o[h + i, :half, :] = dot(tops[i], v[h + i, :half, :], ((1,), (0,)))
            o[h + i, half:, :] = dot(ends[i], v[h + i], ((1,), (0,)))
        turn = h - lag * chip

        @pl.when(jnp.logical_not(first) & jnp.logical_not(last) & (turn >= 0) & (turn < hc))
        def _():
            service(turn)
            service(turn + 1)

    t_last = jnp.where(even, tag_prev[0:1, :], tag_even_row())
    keep[...] = jnp.where(seg_col[...] == t_last, 1.0, 0.0).astype(BF16)

    def add_inter(pieces):
        here = keep[...]
        squares = sq[...]
        for h, state in pieces:
            total = o[h] + dot(q[h] * here, state[...], ((1,), (0,)))
            o[h] = total
            squares = squares + total * total
        sq[...] = squares

    def late_service(j):
        @pl.when(jnp.logical_not(first) & (last | (lag * chip + j >= heads)))
        def _():
            service(j)
            service(j + 1)

    def own_pieces(j):
        return [(mine + j + i, sb_own.at[j + i]) for i in range(2)]

    def other_pieces(j):
        for i in range(2):
            sb_copy(j + i).wait_recv()
        return [(other + j + i, sb_rcv.at[j + i]) for i in range(2)]

    late_service(0)
    add_inter(own_pieces(0))

    @pl.loop(2, hc, step=2)
    def _(j):
        late_service(j)
        add_inter(other_pieces(j - 2) + own_pieces(j))

    add_inter(other_pieces(hc - 2))

    spread = sq[...].T
    ss[0] = jnp.sum(spread.reshape(DH // 8, 8, rows), axis=0)
    for d in range(1, n_head):
        ss_copy(d).start()
    total = ss[0]
    for d in range(1, n_head):
        ss_copy(d).wait_recv()
        total = total + ss[d]
    mean = jnp.sum(total, axis=0, keepdims=True) / (heads * n_head * DH)
    sq[...] = jnp.broadcast_to(lax.rsqrt(mean + EPS), (DH, rows)).T

    for h in range(heads):
        out_ref[:, h * DH:(h + 1) * DH] = (o[h] * sq[...]).astype(BF16)

    tag_pair.wait_send()
    for d in range(1, n_head):
        ss_copy(d).wait_send()

    @pl.when(jnp.logical_not(last))
    def _():
        tag_next.wait_send()

    @pl.loop(0, hc)
    def _(j):
        kv_copy(j).wait_send()
        sb_copy(j).wait_send()

        @pl.when(jnp.logical_not(last))
        def _():
            p_copy(j).wait_send()


def on_device(n_ctx, n_head, queries, keys, values, segment_ids):
    rows, cols = queries.shape
    heads = cols // DH
    hc = heads // 2
    wire = BF16 if n_ctx <= 16 else F32
    vmem, dma = pltpu.VMEM, pltpu.SemaphoreType.DMA
    big = vmem((heads, rows, DH), BF16)
    state = vmem((hc, DH, DH), F32)
    state_p = vmem((hc, DH, DH), wire)
    state_b = vmem((hc, DH, DH), BF16)
    tag = vmem((8, DH), F32)
    anywhere = pl.BlockSpec(memory_space=pl.ANY)
    inside = pl.BlockSpec(memory_space=pltpu.VMEM)
    return pl.pallas_call(
        functools.partial(kernel, n_ctx, n_head),
        out_shape=pltpu.VMEM((rows, cols), BF16),
        in_specs=[anywhere, anywhere, anywhere, anywhere],
        out_specs=inside,
        scratch_shapes=[
            big, big, big,
            vmem((1, rows), jnp.int32),
            vmem((heads, rows, DH), F32),
            vmem((rows, rows), BF16),
            vmem((rows, DH), BF16),
            vmem((rows, DH), F32),
            vmem((rows, DH), F32),
            state, state, state, state_p, state_p, state_b, state_b, state_b,
            tag, tag, tag, tag,
            vmem((n_head, 8, rows), F32),
            dma((3, heads)), dma,
            dma((hc,)), dma((hc,)), dma((hc,)), dma((hc,)), dma((hc,)), dma((hc,)),
            dma((2,)), dma((2,)), dma((n_head,)), dma((n_head,)),
        ],
        compiler_params=pltpu.CompilerParams(
            collective_id=0, has_side_effects=True, vmem_limit_bytes=60 * 2**20
        ),
        cost_estimate=pl.CostEstimate(
            flops=2 * heads * rows * DH * (2 * rows + 2 * DH), bytes_accessed=8 * rows * cols, transcendentals=rows
        ),
    )(queries, keys, values, segment_ids.reshape(1, rows))


def solution(mesh):
    n_ctx, n_head = mesh.shape["ctx"], mesh.shape["head"]
    in_specs = (P("ctx", "head"), P("ctx", "head"), P("ctx", "head"), P("ctx"))
    return jax.shard_map(
        functools.partial(on_device, n_ctx, n_head),
        mesh=mesh, in_specs=in_specs, out_specs=P("ctx", "head"), check_vma=False,
    )
```

```python
import functools

import jax
import jax.numpy as jnp
from jax import lax
from jax.experimental import pallas as pl
from jax.experimental.pallas import tpu as pltpu
from jax.sharding import PartitionSpec as P

DH = 128
EPS = 1e-05
F32 = jnp.float32
BF16 = jnp.bfloat16
MESH = pl.DeviceIdType.MESH


def dot(a, b, dims):
    return lax.dot_general(a, b, (dims, ((), ())), preferred_element_type=F32)


def kernel(
    n_ctx, n_head,
    q_hbm, k_hbm, v_hbm, seg_hbm, out_ref,
    q, k, v, seg, o, mask, keep, seg_col, sq,
    kv_own, kv_send, kv_rcv, p_rcv, p_send, sb_own, sb_send, sb_rcv,
    tag_own, tag_partner, tag_odd, tag_prev, ss,
    in_sem, seg_sem, kv_ssem, kv_rsem, p_ssem, p_rsem, sb_ssem, sb_rsem, tag_ssem, tag_rsem, ss_ssem, ss_rsem,
):
    heads, rows, _ = q.shape
    hc = heads // 2
    half = rows // 2
    chips = n_ctx // 2
    ctx = lax.axis_index("ctx")
    me = lax.axis_index("head")
    core = ctx % 2
    chip = ctx // 2
    even = core == 0
    partner = ctx + 1 - 2 * core
    first, last = chip == 0, chip == chips - 1
    mine, other = core * hc, (1 - core) * hc

    def load(which, h):
        src, dst = ((k_hbm, k), (v_hbm, v), (q_hbm, q))[which]
        cols = pl.ds(pl.multiple_of(h * DH, DH), DH)
        return pltpu.make_async_copy(src.at[:, cols], dst.at[h], in_sem.at[which, h])

    def remote(src, dst, ssem, rsem, where):
        return pltpu.make_async_remote_copy(
            src_ref=src, dst_ref=dst, send_sem=ssem, recv_sem=rsem, device_id=where, device_id_type=MESH
        )

    def kv_copy(j):
        return remote(kv_send.at[j], kv_rcv.at[j], kv_ssem.at[j], kv_rsem.at[j], {"ctx": partner})

    def p_copy(j):
        return remote(p_send.at[j], p_rcv.at[j], p_ssem.at[j], p_rsem.at[j], {"ctx": ctx + 2})

    def sb_copy(j):
        return remote(sb_send.at[j], sb_rcv.at[j], sb_ssem.at[j], sb_rsem.at[j], {"ctx": partner})

    tag_pair = remote(tag_own, tag_partner, tag_ssem.at[0], tag_rsem.at[0], {"ctx": partner})
    tag_next = remote(tag_odd, tag_prev, tag_ssem.at[1], tag_rsem.at[1], {"ctx": ctx + 2})

    def ss_copy(d):
        return remote(ss.at[0], ss.at[d], ss_ssem.at[d], ss_rsem.at[d], {"head": lax.rem(me + d, n_head)})

    seg_load = pltpu.make_async_copy(seg_hbm, seg, seg_sem)
    seg_load.start()

    @pl.loop(0, hc)
    def _(j):
        for base in (other, mine):
            load(0, base + j).start()
            load(1, base + j).start()

    barrier = pltpu.get_barrier_semaphore()
    pl.semaphore_signal(barrier, inc=1, device_id={"ctx": partner}, device_id_type=MESH)
    for d in range(1, n_head):
        pl.semaphore_signal(
            barrier, inc=1, device_id={"head": lax.rem(me + d, n_head)}, device_id_type=MESH
        )

    @pl.when(jnp.logical_not(first))
    def _():
        pl.semaphore_signal(barrier, inc=1, device_id={"ctx": ctx - 2}, device_id_type=MESH)

    @pl.when(jnp.logical_not(last))
    def _():
        pl.semaphore_signal(barrier, inc=1, device_id={"ctx": ctx + 2}, device_id_type=MESH)

    seg_load.wait()
    seg_row = seg[...].astype(F32)
    seg_col[...] = jnp.broadcast_to(seg_row, (DH, rows)).T
    col = seg_col[...]
    tail = col[rows - 1:rows, :]
    tag_own[...] = jnp.broadcast_to(tail, tag_own.shape)
    keep[...] = jnp.where(col == tail, 1.0, 0.0).astype(BF16)
    sq[...] = jnp.zeros_like(sq)

    @pl.when(first)
    def _():
        p_rcv[...] = jnp.zeros_like(p_rcv)
        tag_prev[...] = jnp.full_like(tag_prev, -1.0)

    greeted = n_head + 2 - first.astype(jnp.int32) - last.astype(jnp.int32)
    pl.semaphore_wait(barrier, greeted)
    tag_pair.start()

    def tag_even_row():
        return jnp.where(even, tag_own[0:1, :], tag_partner[0:1, :])

    def service(j):
        kv_copy(j).wait_recv()

        @pl.when(jnp.logical_not(first))
        def _():
            p_copy(j).wait_recv()

        own, got = kv_own[j], kv_rcv[j]
        kv_even = jnp.where(even, own, got)
        kv_odd = jnp.where(even, got, own)
        t_even = tag_even_row()
        stay_even = jnp.where(tag_prev[0:1, :] == t_even, 1.0, 0.0)
        stay_odd = jnp.where(t_even == tag_odd[0:1, :], 1.0, 0.0)
        before = p_rcv[j].astype(F32)
        middle = before * stay_even + kv_even

        @pl.when(jnp.logical_not(last))
        def _():
            p_send[j] = (middle * stay_odd + kv_odd).astype(p_send.dtype)
            p_copy(j).start()

        sb_own[j] = jnp.where(even, before, middle).astype(BF16)
        sb_send[j] = jnp.where(even, middle, before).astype(BF16)
        sb_copy(j).start()

    def kv_step(j):
        ahead = [(base + j + i) for i in range(2) for base in (other, mine)]
        for h in ahead:
            load(0, h).wait()
            load(1, h).wait()
        stay = keep[...]
        sums = [dot(k[h] * stay, v[h], ((0,), (0,))) for h in ahead]
        for i in range(2):
            kv_send[j + i] = sums[2 * i]
            kv_own[j + i] = sums[2 * i + 1]
        for i in range(2):
            kv_copy(j + i).start()

    @pl.loop(0, heads)
    def _(h):
        load(2, h).start()

    kv_step(0)
    tag_pair.wait_recv()
    tag_odd[...] = jnp.where(even, tag_partner[...], tag_own[...])

    @pl.when(jnp.logical_not(last))
    def _():
        tag_next.start()

    @pl.loop(2, hc, step=2)
    def _(j):
        kv_step(j)

        @pl.when(first)
        def _():
            service(j - 2)
            service(j - 1)

    @pl.when(first)
    def _():
        service(hc - 2)
        service(hc - 1)

    @pl.when(jnp.logical_not(first))
    def _():
        tag_next.wait_recv()

    col = seg_col[...]
    seg_row = seg[...].astype(F32)
    t_at = lax.broadcasted_iota(jnp.int32, (rows, DH), 0)
    s_at = lax.broadcasted_iota(jnp.int32, (rows, DH), 1)
    for c in range(rows // DH):
        cut = slice(c * DH, (c + 1) * DH)
        seen = (col == seg_row[:, cut]) & (t_at >= s_at + c * DH)
        mask[:, cut] = jnp.where(seen, 1.0, 0.0).astype(BF16)
    begin = 2 * chip

    @pl.loop(0, heads, step=2)
    def _(h):
        for i in range(2):
            load(2, h + i).wait()
        tops = [dot(q[h + i, :half, :], k[h + i, :half, :], ((1,), (1,))) for i in range(2)]
        ends = [dot(q[h + i, half:, :], k[h + i], ((1,), (1,))) for i in range(2)]
        tops = [part.astype(BF16) * mask[:half, :half] for part in tops]
        ends = [part.astype(BF16) * mask[half:, :] for part in ends]
        for i in range(2):
            o[h + i, :half, :] = dot(tops[i], v[h + i, :half, :], ((1,), (0,)))
            o[h + i, half:, :] = dot(ends[i], v[h + i], ((1,), (0,)))
        turn = h - begin

        @pl.when(jnp.logical_not(first) & jnp.logical_not(last) & (turn >= 0) & (turn < hc))
        def _():
            service(turn)
            service(turn + 1)

    t_last = jnp.where(even, tag_prev[0:1, :], tag_even_row())
    keep[...] = jnp.where(seg_col[...] == t_last, 1.0, 0.0).astype(BF16)

    def add_inter(pieces):
        here = keep[...]
        squares = sq[...]
        for h, state in pieces:
            total = o[h] + dot(q[h] * here, state[...], ((1,), (0,)))
            o[h] = total
            squares = squares + total * total
        sq[...] = squares

    def late_service(j):
        @pl.when(jnp.logical_not(first) & (last | (begin + j >= heads)))
        def _():
            service(j)
            service(j + 1)

    def own_pieces(j):
        return [(mine + j + i, sb_own.at[j + i]) for i in range(2)]

    def other_pieces(j):
        for i in range(2):
            sb_copy(j + i).wait_recv()
        return [(other + j + i, sb_rcv.at[j + i]) for i in range(2)]

    late_service(0)
    add_inter(own_pieces(0))

    @pl.loop(2, hc, step=2)
    def _(j):
        late_service(j)
        add_inter(other_pieces(j - 2) + own_pieces(j))

    add_inter(other_pieces(hc - 2))

    spread = sq[...].T
    ss[0] = jnp.sum(spread.reshape(DH // 8, 8, rows), axis=0)
    for d in range(1, n_head):
        ss_copy(d).start()
    total = ss[0]
    for d in range(1, n_head):
        ss_copy(d).wait_recv()
        total = total + ss[d]
    mean = jnp.sum(total, axis=0, keepdims=True) / (heads * n_head * DH)
    sq[...] = jnp.broadcast_to(lax.rsqrt(mean + EPS), (DH, rows)).T

    for r in range(0, rows, 64):
        scale = sq[r:r + 64, :]
        for h in range(heads):
            out_ref[r:r + 64, h * DH:(h + 1) * DH] = (o[h, r:r + 64, :] * scale).astype(BF16)

    tag_pair.wait_send()
    for d in range(1, n_head):
        ss_copy(d).wait_send()

    @pl.when(jnp.logical_not(last))
    def _():
        tag_next.wait_send()

    @pl.loop(0, hc)
    def _(j):
        kv_copy(j).wait_send()
        sb_copy(j).wait_send()

        @pl.when(jnp.logical_not(last))
        def _():
            p_copy(j).wait_send()


def on_device(n_ctx, n_head, queries, keys, values, segment_ids):
    rows, cols = queries.shape
    heads = cols // DH
    hc = heads // 2
    wire = BF16 if n_ctx <= 16 else F32
    vmem, dma = pltpu.VMEM, pltpu.SemaphoreType.DMA
    big = vmem((heads, rows, DH), BF16)
    state = vmem((hc, DH, DH), F32)
    state_p = vmem((hc, DH, DH), wire)
    state_b = vmem((hc, DH, DH), BF16)
    tag = vmem((8, DH), F32)
    anywhere = pl.BlockSpec(memory_space=pl.ANY)
    inside = pl.BlockSpec(memory_space=pltpu.VMEM)
    return pl.pallas_call(
        functools.partial(kernel, n_ctx, n_head),
        out_shape=pltpu.VMEM((rows, cols), BF16),
        in_specs=[anywhere, anywhere, anywhere, anywhere],
        out_specs=inside,
        scratch_shapes=[
            big, big, big,
            vmem((1, rows), jnp.int32),
            vmem((heads, rows, DH), F32),
            vmem((rows, rows), BF16),
            vmem((rows, DH), BF16),
            vmem((rows, DH), F32),
            vmem((rows, DH), F32),
            state, state, state, state_p, state_p, state_b, state_b, state_b,
            tag, tag, tag, tag,
            vmem((n_head, 8, rows), F32),
            dma((3, heads)), dma,
            dma((hc,)), dma((hc,)), dma((hc,)), dma((hc,)), dma((hc,)), dma((hc,)),
            dma((2,)), dma((2,)), dma((n_head,)), dma((n_head,)),
        ],
        compiler_params=pltpu.CompilerParams(
            collective_id=0, has_side_effects=True, vmem_limit_bytes=60 * 2**20
        ),
        cost_estimate=pl.CostEstimate(
            flops=2 * heads * rows * DH * (2 * rows + 2 * DH), bytes_accessed=8 * rows * cols, transcendentals=rows
        ),
    )(queries, keys, values, segment_ids.reshape(1, rows))


def solution(mesh):
    n_ctx, n_head = mesh.shape["ctx"], mesh.shape["head"]
    in_specs = (P("ctx", "head"), P("ctx", "head"), P("ctx", "head"), P("ctx"))
    return jax.shard_map(
        functools.partial(on_device, n_ctx, n_head),
        mesh=mesh, in_specs=in_specs, out_specs=P("ctx", "head"), check_vma=False,
    )
```
